32 devices in a mesh: dp: 4 (over y, x), fsdp: 8 (over z, core).
Axes of the slice: x: 2, y: 2, z: 4, core: 2. Of those that a mesh axis runs over, the one named last changes fastest.
Arguments:
- tokens: bfloat16 [4096, 3072], P(('dp', 'fsdp')), may hold values from -6 to 6
- hess_tokens: bfloat16 [1024, 3072], P(('dp', 'fsdp')), may hold values from -6 to 6
- upstream: bfloat16 [4096, 12288], P('dp', 'fsdp'), may hold values from -5 to 5
- hess_upstream: bfloat16 [1024, 12288], P('dp', 'fsdp'), may hold values from -0.75 to 0.75
- weight: bfloat16 [3072, 12288], P(None, 'fsdp'), may hold values from -0.109375 to 0.109375
- probes: bfloat16 [3072, 12288], P('dp', 'fsdp'), may hold values from -6 to 6
- momentum: float32 [3072, 12288], P('dp', 'fsdp'), may hold values from -0.3 to 0.3
- curvature: float32 [3072, 12288], P('dp', 'fsdp'), may hold values from 0.1 to 10
Outputs:
- new_weight: bfloat16 [3072, 12288], P('dp', 'fsdp')
- new_momentum: float32 [3072, 12288], P('dp', 'fsdp')
- new_curvature: float32 [3072, 12288], P('dp', 'fsdp')
The draws below stay inside these ranges and needn't reach their ends.
All inputs are finite; a program needn't handle non-finite values.
Results may differ from the reference program's by a relative error of at most 0.015.
Values may be sent and summed in bfloat16 or wider, within the bound.
A program may use at most 128 MiB of HBM per device.

```python
import math
import jax
import jax.numpy as jnp
from jax import lax

D = 3072
FF = 12288
TOK_DEV = 128
HESS_DEV = 32
TOKENS = 4096
HTOKENS = 1024
N_DP = 4
N_FSDP = 8


def steps_of(stream_key, shape, pieces, low, largest):
    gain = 1.0
    for axis_at, blocks in pieces:
        heights = jax.random.uniform(jax.random.fold_in(jax.random.fold_in(stream_key, 6), axis_at), (blocks,), jnp.float32, low / len(pieces), largest / len(pieces))
        gain = gain * jnp.repeat(jnp.exp(heights), shape[axis_at] // blocks).reshape((-1,) + (1,) * (len(shape) - 1 - axis_at))
    return gain


def normal_values(own_key, extent, scale, bound, split=(), kind=jnp.bfloat16):
    factor_of = steps_of(own_key, extent, split, -0.22, 0.18) if split else 1.0
    result = jax.random.normal(own_key, extent, jnp.float32) * scale * factor_of
    return jnp.minimum(jnp.maximum(result, -bound), bound).astype(kind)


def setup_inputs(seed: int = 0) -> dict:
    seeds = jax.random.split(jax.random.key(seed), 9)
    return {
        "tokens": normal_values(seeds[0], (TOKENS, D), 1.0, 6.0, ((0, 32),)),
        "hess_tokens": normal_values(seeds[1], (HTOKENS, D), 1.0, 6.0, ((0, 32),)),
        "upstream": normal_values(seeds[2], (TOKENS, FF), (4 * TOK_DEV ** -0.5), 5.0, ((0, 4), (1, 8))),
        "hess_upstream": normal_values(seeds[3], (HTOKENS, FF), (16 * HESS_DEV ** -0.5 * D ** -0.5), 0.75, ((0, 4), (1, 8))),
        "weight": normal_values(seeds[4], (D, FF), D ** -0.5, 0.109375, ((1, 8),)),
        "probes": normal_values(seeds[5], (D, FF), 1.0, 6.0, ((0, 4), (1, 8))),
        "momentum": normal_values(seeds[6], (D, FF), 0.05, 0.3, ((0, 4), (1, 8)), jnp.float32),
        "curvature": jnp.clip(jnp.exp(math.log(10.0) - 4.6051702 * jax.random.uniform(seeds[7], (D, FF), jnp.float32) ** steps_of(seeds[7], (D, FF), ((0, 4), (1, 8)), -0.2, 0.2)), 0.1, 10.0),
    }


SQRT_HALF = 1.0 / math.sqrt(2.0)
INV_ROOT_TAU = 1.0 / math.sqrt(2.0 * math.pi)
BETA_ONE = 0.965
BETA_TWO = 0.99
LEARN_RATE = 0.0006
WEIGHT_DECAY = 0.1
HESS_SCALE = 0.01
RATIO_FLOOR = 0.001

def gelu_slope(preact):
    normal_cdf = 0.5 * (1.0 + jax.scipy.special.erf(preact * SQRT_HALF))
    density = jnp.exp(-0.5 * preact * preact) * INV_ROOT_TAU
    return normal_cdf + preact * density

def gelu_bend(preact):
    density = jnp.exp(-0.5 * preact * preact) * INV_ROOT_TAU
    return density * (2.0 - preact * preact)

def rounded(value):
    narrow = lax.optimization_barrier(value.astype(jnp.bfloat16))
    return narrow.astype(jnp.float32)

def reference(tokens, hess_tokens, upstream, hess_upstream, weight, probes, momentum, curvature):
    group_rows = TOK_DEV * N_FSDP
    hess_rows = HESS_DEV * N_FSDP
    gradient = jnp.zeros((D, FF), jnp.float32)
    hessian_vec = jnp.zeros((D, FF), jnp.float32)
    for replica in range(N_DP):
        batch_rows = tokens[replica * group_rows:(replica + 1) * group_rows]
        signal = upstream[replica * group_rows:(replica + 1) * group_rows]
        preact = jnp.dot(batch_rows, weight, preferred_element_type=jnp.float32)
        slopes = (signal.astype(jnp.float32) * gelu_slope(preact)).astype(jnp.bfloat16)
        gradient = gradient + rounded(jnp.dot(batch_rows.T, slopes, preferred_element_type=jnp.float32))
        hess_block = hess_tokens[replica * hess_rows:(replica + 1) * hess_rows]
        hess_signal = hess_upstream[replica * hess_rows:(replica + 1) * hess_rows]
        hess_pre = jnp.dot(hess_block, weight, preferred_element_type=jnp.float32)
        tangent = jnp.dot(hess_block, probes, preferred_element_type=jnp.float32)
        curved = (hess_signal.astype(jnp.float32) * gelu_bend(hess_pre) * tangent).astype(jnp.bfloat16)
        hessian_vec = hessian_vec + rounded(jnp.dot(hess_block.T, curved, preferred_element_type=jnp.float32))
    new_curvature = BETA_TWO * curvature + (1.0 - BETA_TWO) * (probes.astype(jnp.float32) * hessian_vec)
    new_momentum = BETA_ONE * momentum + (1.0 - BETA_ONE) * gradient
    ratio = jnp.clip(new_momentum / jnp.maximum(HESS_SCALE * new_curvature, RATIO_FLOOR), -1.0, 1.0)
    new_weight = (weight.astype(jnp.float32) * (1.0 - LEARN_RATE * WEIGHT_DECAY) - LEARN_RATE * ratio).astype(jnp.bfloat16)
    return (new_weight, new_momentum, new_curvature)
```

```python
import functools
import math

import jax
import jax.numpy as jnp
from jax import lax
from jax.experimental import pallas as pl
from jax.experimental.pallas import tpu as pltpu
from jax.sharding import PartitionSpec as P

SQRT_HALF = 1.0 / math.sqrt(2.0)
INV_ROOT_TAU = 1.0 / math.sqrt(2.0 * math.pi)
BETA_ONE = 0.965
BETA_TWO = 0.99
LEARN_RATE = 0.0006
WEIGHT_DECAY = 0.1
HESS_SCALE = 0.01
RATIO_FLOOR = 0.001
VMEM_BYTES = 48 * 1024 * 1024
F32, BF16 = jnp.float32, jnp.bfloat16


def gelu_slope(preact):
    normal_cdf = 0.5 * (1.0 + jax.scipy.special.erf(preact * SQRT_HALF))
    density = jnp.exp(-0.5 * preact * preact) * INV_ROOT_TAU
    return normal_cdf + preact * density


def gelu_bend(preact):
    density = jnp.exp(-0.5 * preact * preact) * INV_ROOT_TAU
    return density * (2.0 - preact * preact)


def row_contract(left, right):
    return lax.dot_general(left, right, (((0,), (0,)), ((), ())), preferred_element_type=F32)


def swap(value, axis, bit):
    count = lax.axis_size(axis)
    return lax.ppermute(value, axis, [(i, i ^ bit) for i in range(count)])


def bit_orders(count):
    bits = [1 << k for k in range(count.bit_length() - 1)]
    return bits, bits[::-1]


def scatter_terms(parts, bits):
    parts = {j: ([v] if j == 0 else v) for j, v in parts.items()}
    for at, bit in enumerate(bits):
        later = sum(bits[at + 1:])
        for j in sorted((j for j in parts if j & bit), key=lambda j: -(j & later)):
            arrived = swap(parts.pop(j), "dp", bit)
            if j == bit:
                parts[0] = parts[0] + [arrived]
            else:
                parts[j ^ bit] = (parts[j ^ bit].astype(F32) + arrived.astype(F32)).astype(BF16)
    return parts[0]


def gather_all(value, bits):
    held = {0: value}
    for bit in bits:
        held.update({j ^ bit: swap(v, "dp", bit) for j, v in list(held.items())})
    return held


def contract_body(count, owners_ref, *refs):
    total = row_contract(refs[0][...], refs[count][...])
    for k in range(1, count):
        total = total + row_contract(refs[k][...], refs[count + k][...])
    refs[2 * count][0] = total.astype(BF16)


def grad_blocks(owners, lefts, rights, owned, half, side):
    count, blocks = len(lefts), owners.shape[0]
    tile = math.gcd(owned, 384)
    per = owned // tile
    depth = lefts[0].shape[0]
    return pl.pallas_call(
        functools.partial(contract_body, count),
        grid_spec=pltpu.PrefetchScalarGridSpec(
            num_scalar_prefetch=1,
            grid=(blocks, per),
            in_specs=[pl.BlockSpec((depth, tile), lambda b, m, o: (0, o[b] * per + m))] * count
            + [pl.BlockSpec((depth, half), lambda b, m, o: (0, side))] * count,
            out_specs=pl.BlockSpec((1, tile, half), lambda b, m, o: (b, m, 0)),
        ),
        out_shape=jax.ShapeDtypeStruct((blocks, owned, half), BF16),
        compiler_params=pltpu.CompilerParams(vmem_limit_bytes=VMEM_BYTES),
        cost_estimate=pl.CostEstimate(
            flops=2 * blocks * owned * half * depth * count,
            bytes_accessed=2 * (blocks * owned * half + depth * count * (blocks * owned + half)),
            transcendentals=0,
        ),
    )(owners, *lefts, *rights)


def curvature_body(count, probes_ref, curv_ref, *refs):
    total = row_contract(refs[0][...], refs[count][...])
    for k in range(1, count):
        total = total + row_contract(refs[k][...], refs[count + k][...])
    refs[2 * count][...] = BETA_TWO * curv_ref[...] + (1.0 - BETA_TWO) * (
        probes_ref[...].astype(F32) * total
    )


def curvature_step(probes, curvature, lefts, rights):
    owned, width = probes.shape
    count, depth = len(lefts), lefts[0].shape[0]
    tile = math.gcd(owned, 128)
    rows = pl.BlockSpec((tile, width), lambda m: (m, 0))
    return pl.pallas_call(
        functools.partial(curvature_body, count),
        grid=(owned // tile,),
        in_specs=[rows, rows]
        + [pl.BlockSpec((depth, tile), lambda m: (0, m))] * count
        + [pl.BlockSpec((depth, width), lambda m: (0, 0))] * count,
        out_specs=rows,
        out_shape=jax.ShapeDtypeStruct((owned, width), F32),
        compiler_params=pltpu.CompilerParams(vmem_limit_bytes=VMEM_BYTES),
        cost_estimate=pl.CostEstimate(
            flops=2 * owned * width * depth * count, bytes_accessed=12 * owned * width, transcendentals=0
        ),
    )(probes, curvature, *lefts, *rights)


def update_body(terms, half, owner_ref, weight_ref, mom_ref, curv_ref, *refs):
    out_weight, out_mom = refs[2 * terms:]
    for side in range(2):
        cols = slice(side * half, (side + 1) * half)
        pieces = refs[side * terms:(side + 1) * terms]
        gradient = pieces[0][...].astype(F32)
        for piece in pieces[1:]:
            gradient = gradient + piece[...].astype(F32)
        new_mom = BETA_ONE * mom_ref[:, cols] + (1.0 - BETA_ONE) * gradient
        floor = jnp.maximum(HESS_SCALE * curv_ref[:, cols], RATIO_FLOOR)
        ratio = jnp.clip(new_mom / floor, -1.0, 1.0)
        out_mom[:, cols] = new_mom
        out_weight[:, cols] = (
            weight_ref[:, cols].astype(F32) * (1.0 - LEARN_RATE * WEIGHT_DECAY) - LEARN_RATE * ratio
        ).astype(BF16)


def update_step(owner, weight, momentum, new_curvature, first, second):
    owned, width = momentum.shape
    half, terms = width // 2, len(first)
    tile = math.gcd(owned, 128)
    per = owned // tile
    rows = pl.BlockSpec((tile, width), lambda m, o: (m, 0))
    return pl.pallas_call(
        functools.partial(update_body, terms, half),
        grid_spec=pltpu.PrefetchScalarGridSpec(
            num_scalar_prefetch=1,
            grid=(per,),
            in_specs=[pl.BlockSpec((tile, width), lambda m, o: (o[0] * per + m, 0)), rows, rows]
            + [pl.BlockSpec((tile, half), lambda m, o: (m, 0))] * (2 * terms),
            out_specs=[rows, rows],
        ),
        out_shape=[
            jax.ShapeDtypeStruct((owned, width), BF16),
            jax.ShapeDtypeStruct((owned, width), F32),
        ],
        compiler_params=pltpu.CompilerParams(vmem_limit_bytes=VMEM_BYTES),
        cost_estimate=pl.CostEstimate(
            flops=10 * owned * width, bytes_accessed=22 * owned * width, transcendentals=0
        ),
    )(owner, weight, momentum, new_curvature, *first, *second)


def shards(tokens, hess_tokens, upstream, hess_upstream, weight, probes, momentum, curvature):
    n_dp, n_fsdp = lax.axis_size("dp"), lax.axis_size("fsdp")
    own, lane = lax.axis_index("dp"), lax.axis_index("fsdp")
    owned, width = probes.shape
    half = width // 2
    forward, backward = bit_orders(n_dp)
    sides = ((0, forward), (1, backward))

    all_hess = lax.all_gather(hess_tokens, "fsdp", axis=0, tiled=True)
    columns = {
        j: lax.dynamic_slice_in_dim(all_hess, (own ^ j) * owned, owned, 1) for j in range(n_dp)
    }
    hess_cols = {0: columns[0]}
    for j in range(1, n_dp):
        hess_cols[j] = swap(columns[j], "dp", j)

    chips = n_fsdp // 2
    ring = [p for p in range(0, chips, 2)] + [p for p in range(1, chips, 2)][::-1]
    place = {p: k for k, p in enumerate(ring)}
    steps = [
        (2 * p + c, 2 * ring[(place[p] + 1) % chips] + c) for p in range(chips) for c in range(2)
    ]
    spot = jnp.zeros((), jnp.int32)
    for p in range(chips):
        spot = spot + jnp.where(lane // 2 == p, place[p], 0).astype(jnp.int32)
    token_rows = tokens.shape[0]
    held = tokens
    token_chunks, slope_chunks = [], []
    for k in range(chips):
        at = (spot - k) % chips
        origin = jnp.zeros((), jnp.int32)
        for p in range(chips):
            origin = origin + jnp.where(at == place[p], p, 0).astype(jnp.int32)
        other = swap(held, "fsdp", 1)
        first = jnp.where(lane % 2 == 0, held, other)
        second = jnp.where(lane % 2 == 0, other, held)
        chunk = jnp.concatenate([first, second], axis=0)
        signal = lax.dynamic_slice_in_dim(upstream, origin * 2 * token_rows, 2 * token_rows, 0)
        preact = jnp.dot(chunk, weight, preferred_element_type=F32)
        slope_chunks.append((signal.astype(F32) * gelu_slope(preact)).astype(BF16))
        token_chunks.append(chunk)
        if k < chips - 1:
            held = lax.ppermute(held, "fsdp", steps)

    tangents = {
        j: jnp.dot(hess_cols[j], probes, preferred_element_type=F32).astype(BF16)
        for j in range(n_dp)
    }
    tangent_sides = []
    for side, bits in sides:
        part = {j: v[:, side * half:(side + 1) * half] for j, v in tangents.items()}
        terms = scatter_terms(part, bits)
        tangent_sides.append(sum(t.astype(F32) for t in terms))
    hess_pre = jnp.dot(all_hess, weight, preferred_element_type=F32)
    curved_sides = []
    for side, bits in sides:
        cols = slice(side * half, (side + 1) * half)
        curved = (
            hess_upstream[:, cols].astype(F32) * gelu_bend(hess_pre[:, cols]) * tangent_sides[side]
        ).astype(BF16)
        curved_sides.append(gather_all(curved, bits))
    curved_all = [
        jnp.concatenate([curved_sides[0][j], curved_sides[1][j]], axis=1) for j in range(n_dp)
    ]
    new_curvature = curvature_step(
        probes, curvature, [hess_cols[j] for j in range(n_dp)], curved_all
    )

    grad_terms = []
    shares = []
    for side, bits in sides:
        out_list = [j for j in range(n_dp) if j & bits[0]]
        out_list.sort(key=lambda j: -(j & ~bits[0]))
        owners = jnp.stack([own ^ j for j in out_list]).astype(jnp.int32)
        sent = grad_blocks(owners, token_chunks, slope_chunks, owned, half, side)
        shares.append({j: sent[k] for k, j in enumerate(out_list)})
    for side, bits in sides:
        keep_list = [j for j in range(n_dp) if not j & bits[0]][::-1]
        owners = jnp.stack([own ^ j for j in keep_list]).astype(jnp.int32)
        kept = grad_blocks(owners, token_chunks, slope_chunks, owned, half, side)
        shares[side].update({j: kept[k] for k, j in enumerate(keep_list)})
        grad_terms.append(scatter_terms(shares[side], bits))

    new_weight, new_momentum = update_step(
        own.astype(jnp.int32).reshape((1,)), weight, momentum, new_curvature, *grad_terms
    )
    return (new_weight, new_momentum, new_curvature)


def solution(mesh):
    return jax.shard_map(
        shards,
        mesh=mesh,
        in_specs=(
            P(("dp", "fsdp"), None),
            P(("dp", "fsdp"), None),
            P("dp", "fsdp"),
            P("dp", "fsdp"),
            P(None, "fsdp"),
            P("dp", "fsdp"),
            P("dp", "fsdp"),
            P("dp", "fsdp"),
        ),
        out_specs=(P("dp", "fsdp"), P("dp", "fsdp"), P("dp", "fsdp")),
        check_vma=False,
    )
```

```python
import functools
import math

import jax
import jax.numpy as jnp
from jax import lax
from jax.experimental import pallas as pl
from jax.experimental.pallas import tpu as pltpu
from jax.sharding import PartitionSpec as P

SQRT_HALF = 1.0 / math.sqrt(2.0)
INV_ROOT_TAU = 1.0 / math.sqrt(2.0 * math.pi)
BETA_ONE = 0.965
BETA_TWO = 0.99
LEARN_RATE = 0.0006
WEIGHT_DECAY = 0.1
HESS_SCALE = 0.01
RATIO_FLOOR = 0.001
VMEM_BYTES = 48 * 1024 * 1024
F32, BF16 = jnp.float32, jnp.bfloat16


def gelu_slope(preact):
    normal_cdf = 0.5 * (1.0 + jax.scipy.special.erf(preact * SQRT_HALF))
    density = jnp.exp(-0.5 * preact * preact) * INV_ROOT_TAU
    return normal_cdf + preact * density


def gelu_bend(preact):
    density = jnp.exp(-0.5 * preact * preact) * INV_ROOT_TAU
    return density * (2.0 - preact * preact)


def row_contract(left, right):
    return lax.dot_general(left, right, (((0,), (0,)), ((), ())), preferred_element_type=F32)


def swap(value, axis, bit):
    count = lax.axis_size(axis)
    return lax.ppermute(value, axis, [(i, i ^ bit) for i in range(count)])


def bit_orders(count):
    bits = [1 << k for k in range(count.bit_length() - 1)]
    return bits, bits[::-1]


def scatter_terms(parts, bits):
    parts = {j: ([v] if j == 0 else v) for j, v in parts.items()}
    for at, bit in enumerate(bits):
        later = sum(bits[at + 1:])
        for j in sorted((j for j in parts if j & bit), key=lambda j: -(j & later)):
            arrived = swap(parts.pop(j), "dp", bit)
            if j == bit:
                parts[0] = parts[0] + [arrived]
            else:
                parts[j ^ bit] = (parts[j ^ bit].astype(F32) + arrived.astype(F32)).astype(BF16)
    return parts[0]


def gather_all(value, bits):
    held = {0: value}
    for bit in bits:
        held.update({j ^ bit: swap(v, "dp", bit) for j, v in list(held.items())})
    return held


def contract_body(count, owners_ref, *refs):
    total = row_contract(refs[0][...], refs[count][...])
    for k in range(1, count):
        total = total + row_contract(refs[k][...], refs[count + k][...])
    refs[2 * count][...] = total.astype(BF16)


def grad_block(owner, lefts, rights, owned, half, side):
    count, depth = len(lefts), lefts[0].shape[0]
    tile = math.gcd(owned, 384)
    per = owned // tile
    return pl.pallas_call(
        functools.partial(contract_body, count),
        grid_spec=pltpu.PrefetchScalarGridSpec(
            num_scalar_prefetch=1,
            grid=(per,),
            in_specs=[pl.BlockSpec((depth, tile), lambda m, o: (0, o[0] * per + m))] * count
            + [pl.BlockSpec((depth, half), lambda m, o: (0, side))] * count,
            out_specs=pl.BlockSpec((tile, half), lambda m, o: (m, 0)),
        ),
        out_shape=jax.ShapeDtypeStruct((owned, half), BF16),
        compiler_params=pltpu.CompilerParams(vmem_limit_bytes=VMEM_BYTES),
        cost_estimate=pl.CostEstimate(
            flops=2 * owned * half * depth * count,
            bytes_accessed=2 * (owned * half + depth * count * (owned + half)),
            transcendentals=0,
        ),
    )(owner.astype(jnp.int32).reshape((1,)), *lefts, *rights)


def curvature_body(count, probes_ref, curv_ref, *refs):
    total = row_contract(refs[0][...], refs[count][...])
    for k in range(1, count):
        total = total + row_contract(refs[k][...], refs[count + k][...])
    refs[2 * count][...] = BETA_TWO * curv_ref[...] + (1.0 - BETA_TWO) * (
        probes_ref[...].astype(F32) * total
    )


def curvature_step(probes, curvature, lefts, rights):
    owned, width = probes.shape
    count, depth = len(lefts), lefts[0].shape[0]
    tile = math.gcd(owned, 128)
    rows = pl.BlockSpec((tile, width), lambda m: (m, 0))
    return pl.pallas_call(
        functools.partial(curvature_body, count),
        grid=(owned // tile,),
        in_specs=[rows, rows]
        + [pl.BlockSpec((depth, tile), lambda m: (0, m))] * count
        + [pl.BlockSpec((depth, width), lambda m: (0, 0))] * count,
        out_specs=rows,
        out_shape=jax.ShapeDtypeStruct((owned, width), F32),
        compiler_params=pltpu.CompilerParams(vmem_limit_bytes=VMEM_BYTES),
        cost_estimate=pl.CostEstimate(
            flops=2 * owned * width * depth * count, bytes_accessed=12 * owned * width, transcendentals=0
        ),
    )(probes, curvature, *lefts, *rights)


def update_body(terms, half, owner_ref, weight_ref, mom_ref, curv_ref, *refs):
    out_weight, out_mom = refs[2 * terms:]
    for side in range(2):
        cols = slice(side * half, (side + 1) * half)
        pieces = refs[side * terms:(side + 1) * terms]
        gradient = pieces[0][...].astype(F32)
        for piece in pieces[1:]:
            gradient = gradient + piece[...].astype(F32)
        new_mom = BETA_ONE * mom_ref[:, cols] + (1.0 - BETA_ONE) * gradient
        floor = jnp.maximum(HESS_SCALE * curv_ref[:, cols], RATIO_FLOOR)
        ratio = jnp.clip(new_mom / floor, -1.0, 1.0)
        out_mom[:, cols] = new_mom
        out_weight[:, cols] = (
            weight_ref[:, cols].astype(F32) * (1.0 - LEARN_RATE * WEIGHT_DECAY) - LEARN_RATE * ratio
        ).astype(BF16)


def update_step(owner, weight, momentum, new_curvature, first, second):
    owned, width = momentum.shape
    half, terms = width // 2, len(first)
    tile = math.gcd(owned, 128)
    per = owned // tile
    rows = pl.BlockSpec((tile, width), lambda m, o: (m, 0))
    return pl.pallas_call(
        functools.partial(update_body, terms, half),
        grid_spec=pltpu.PrefetchScalarGridSpec(
            num_scalar_prefetch=1,
            grid=(per,),
            in_specs=[pl.BlockSpec((tile, width), lambda m, o: (o[0] * per + m, 0)), rows, rows]
            + [pl.BlockSpec((tile, half), lambda m, o: (m, 0))] * (2 * terms),
            out_specs=[rows, rows],
        ),
        out_shape=[
            jax.ShapeDtypeStruct((owned, width), BF16),
            jax.ShapeDtypeStruct((owned, width), F32),
        ],
        compiler_params=pltpu.CompilerParams(vmem_limit_bytes=VMEM_BYTES),
        cost_estimate=pl.CostEstimate(
            flops=10 * owned * width, bytes_accessed=22 * owned * width, transcendentals=0
        ),
    )(owner, weight, momentum, new_curvature, *first, *second)


def shards(tokens, hess_tokens, upstream, hess_upstream, weight, probes, momentum, curvature):
    n_dp, n_fsdp = lax.axis_size("dp"), lax.axis_size("fsdp")
    own, lane = lax.axis_index("dp"), lax.axis_index("fsdp")
    owned, width = probes.shape
    half = width // 2
    forward, backward = bit_orders(n_dp)
    sides = ((0, forward), (1, backward))

    hess_rows = hess_tokens.shape[0]
    near = {0: hess_tokens}
    for j in range(2, n_fsdp, 2):
        near[j] = swap(hess_tokens, "fsdp", j)
    chip_rows = jnp.concatenate([near[j] for j in range(0, n_fsdp, 2)], axis=0)
    all_hess = jnp.concatenate([chip_rows, swap(chip_rows, "fsdp", 1)], axis=0)
    order = [j for j in range(0, n_fsdp, 2)] + [j + 1 for j in range(0, n_fsdp, 2)]
    hess_signal = jnp.concatenate(
        [
            lax.dynamic_slice_in_dim(hess_upstream, (lane ^ j) * hess_rows, hess_rows, 0)
            for j in order
        ],
        axis=0,
    )
    columns = [
        lax.dynamic_slice_in_dim(all_hess, (own ^ j) * owned, owned, 1) for j in range(n_dp)
    ]

    chips = n_fsdp // 2
    ring = [p for p in range(0, chips, 2)] + [p for p in range(1, chips, 2)][::-1]
    place = {p: k for k, p in enumerate(ring)}
    steps = [
        (2 * p + c, 2 * ring[(place[p] + 1) % chips] + c) for p in range(chips) for c in range(2)
    ]
    spot = jnp.zeros((), jnp.int32)
    for p in range(chips):
        spot = spot + jnp.where(lane // 2 == p, place[p], 0).astype(jnp.int32)
    token_rows = tokens.shape[0]
    held = tokens
    token_chunks, slope_chunks = [], []
    tangents = None
    for k in range(chips):
        if k == 1:
            held, columns = lax.optimization_barrier((held, columns))
            hess_cols = [columns[0]] + [swap(columns[j], "dp", j) for j in range(1, n_dp)]
        later = lax.ppermute(held, "fsdp", steps) if k < chips - 1 else None
        if k == 2:
            tangents = [
                jnp.dot(v, probes, preferred_element_type=F32).astype(BF16) for v in hess_cols
            ]
            held, tangents = lax.optimization_barrier((held, tangents))
        at = (spot - k) % chips
        origin = jnp.zeros((), jnp.int32)
        for p in range(chips):
            origin = origin + jnp.where(at == place[p], p, 0).astype(jnp.int32)
        other = swap(held, "fsdp", 1)
        first = jnp.where(lane % 2 == 0, held, other)
        second = jnp.where(lane % 2 == 0, other, held)
        chunk = jnp.concatenate([first, second], axis=0)
        signal = lax.dynamic_slice_in_dim(upstream, origin * 2 * token_rows, 2 * token_rows, 0)
        preact = jnp.dot(chunk, weight, preferred_element_type=F32)
        slope_chunks.append((signal.astype(F32) * gelu_slope(preact)).astype(BF16))
        token_chunks.append(chunk)
        held = later

    tangent_sides = []
    for side, bits in sides:
        part = {j: v[:, side * half:(side + 1) * half] for j, v in enumerate(tangents)}
        terms = scatter_terms(part, bits)
        tangent_sides.append(sum(t.astype(F32) for t in terms))
    hess_pre = jnp.dot(all_hess, weight, preferred_element_type=F32)
    curved_own, curved_sides = [], []
    for side, bits in sides:
        cols = slice(side * half, (side + 1) * half)
        curved = (
            hess_signal[:, cols].astype(F32) * gelu_bend(hess_pre[:, cols]) * tangent_sides[side]
        ).astype(BF16)
        curved_own.append(curved)
    curved_own, slope_chunks[-1] = lax.optimization_barrier((curved_own, slope_chunks[-1]))
    for side, bits in sides:
        curved_sides.append(gather_all(curved_own[side], bits))
    curved_all = [
        jnp.concatenate([curved_sides[0][j], curved_sides[1][j]], axis=1) for j in range(n_dp)
    ]
    new_curvature = curvature_step(
        probes, curvature, hess_cols, curved_all
    )

    shares = [{}, {}]
    for j in sorted(range(n_dp), key=lambda j: -j):
        for side, bits in sides:
            flip = sum(b for b, c in zip(bits[::-1], forward) if j & c)
            shares[side][flip] = grad_block(
                own ^ flip, token_chunks, slope_chunks, owned, half, side
            )
    grad_terms = [scatter_terms(shares[side], bits) for side, bits in sides]

    new_weight, new_momentum = update_step(
        own.astype(jnp.int32).reshape((1,)), weight, momentum, new_curvature, *grad_terms
    )
    return (new_weight, new_momentum, new_curvature)


def solution(mesh):
    return jax.shard_map(
        shards,
        mesh=mesh,
        in_specs=(
            P(("dp", "fsdp"), None),
            P(("dp", "fsdp"), None),
            P("dp", "fsdp"),
            P("dp", "fsdp"),
            P(None, "fsdp"),
            P("dp", "fsdp"),
            P("dp", "fsdp"),
            P("dp", "fsdp"),
        ),
        out_specs=(P("dp", "fsdp"), P("dp", "fsdp"), P("dp", "fsdp")),
        check_vma=False,
    )
```
